128 devices in a mesh: leaf: 128 (over y, z, x, core).
Axes of the slice: x: 4, y: 4, z: 4, core: 2. Of those that a mesh axis runs over, the one named last changes fastest.
Arguments:
- rhs: bfloat16 [16, 1048576], P(None, 'leaf'), may hold values from -6 to 6
- leaf_basis: bfloat16 [4096, 256, 64], P('leaf'), may hold values from -0.375 to 0.375
- near_tiles: bfloat16 [4096, 4, 256, 256], P('leaf'), may hold values from -0.375 to 0.375
- near_pairs: int32 [4096, 4], P('leaf'), may hold values from 0 to 4095, as said below
- local_transfer: bfloat16 [7936, 64, 64], P('leaf'), may hold values from -0.625 to 0.625
- local_coupling: bfloat16 [7936, 64, 64], P('leaf'), may hold values from -0.75 to 0.75
- upper_transfer: bfloat16 [252, 64, 64], replicated, may hold values from -0.625 to 0.625
- upper_coupling: bfloat16 [254, 64, 64], replicated, may hold values from -0.75 to 0.75
Outputs:
- product: float32 [16, 1048576], P(None, 'leaf')
The draws below stay inside these ranges and needn't reach their ends.
Inputs may be any that keep to these rules, and one draw needn't show every extreme that they name: near_pairs[n, 0] is n; every entry lies within 32 leaves of n, and entry 1 lies exactly 32 leaves away.
All inputs are finite; a program needn't handle non-finite values.
Results may differ from the reference program's by a relative error of at most 0.0003.
Values may be sent and summed in bfloat16 or wider, within the bound.
No kernel may reach another device: no remote copies, remote signals or barrier semaphores. Data moves between devices by JAX's collectives and lax.ppermute only.
A program may use at most 128 MiB of HBM per device.

```python
import jax
import jax.numpy as jnp
from jax import lax

LEAF_SIZE = 256
RANK = 64
RHS = 16
NEAR_PER = 4
LEAF_DEV = 32
LEAVES = 4096
UNKNOWNS = 1048576
LOCAL_LEVELS = 5
UP_LEVELS = 7
N_LEAF = 128


def draw_near_pairs(key, part):
    key = jax.random.fold_in(key, 11)
    keys = jax.random.split(key, 2)
    leaf_ids = jnp.arange(LEAVES, dtype=jnp.int32)[:, None]
    signs = 2 * jax.random.randint(keys[0], (LEAVES, NEAR_PER - 1), 0, 2) - 1
    reach = jax.random.randint(keys[1], (LEAVES, NEAR_PER - 1), 1, LEAF_DEV + 1)
    reach = reach.at[:, 0].set(LEAF_DEV)
    offsets = (signs * reach).astype(jnp.int32)
    targets = leaf_ids + offsets
    inside = (targets >= 0) & (targets < LEAVES)
    targets = jnp.where(inside, targets, leaf_ids - offsets)
    return jnp.concatenate([leaf_ids, targets], axis=1).astype(jnp.int32)


def levels(key, shape, cuts, least, high):
    level, own = 1.0, jax.random.fold_in(key, 6)
    for position, shards_of in cuts:
        steps = jnp.exp(jax.random.uniform(jax.random.fold_in(own, position), (shards_of,), jnp.float32, least / len(cuts), high / len(cuts)))
        level = level * jnp.repeat(steps, shape[position] // shards_of).reshape([-1 if axis == position else 1 for axis in range(len(shape))])
    return level


def centred(stream_key, extent, width, most, shards=(), kind=jnp.bfloat16):
    values = width * jax.random.normal(stream_key, extent, jnp.float32)
    if shards:
        values = values * levels(stream_key, extent, shards, -0.22, 0.18)
    return jnp.clip(values, -most, most).astype(kind)


def setup_inputs(seed: int = 0) -> dict:
    key_list = jax.random.split(jax.random.key(seed), 9)
    return {
        "rhs": centred(key_list[0], (RHS, UNKNOWNS), 1.0, 6.0, ((1, 128),)),
        "leaf_basis": centred(key_list[1], (LEAVES, LEAF_SIZE, RANK), LEAF_SIZE ** -0.5, 0.375, ((0, 128),)),
        "near_tiles": centred(key_list[2], (LEAVES, NEAR_PER, LEAF_SIZE, LEAF_SIZE), LEAF_SIZE ** -0.5, 0.375, ((0, 128),)),
        "near_pairs": draw_near_pairs(jax.random.fold_in(key_list[8], 71), 0),
        "local_transfer": centred(key_list[4], (N_LEAF * (2 * LEAF_DEV - 2), RANK, RANK), (3 * RANK // 2) ** -0.5, 0.625, ((0, 128),)),
        "local_coupling": centred(key_list[5], (N_LEAF * (2 * LEAF_DEV - 2), RANK, RANK), RANK ** -0.5, 0.75, ((0, 128),)),
        "upper_transfer": centred(key_list[6], (2 * N_LEAF - 4, RANK, RANK), (3 * RANK // 2) ** -0.5, 0.625),
        "upper_coupling": centred(key_list[7], (2 * N_LEAF - 2, RANK, RANK), RANK ** -0.5, 0.75),
    }


def apply_transfer(coefficients, matrices):
    return jnp.einsum("nrk,nkj->nrj", coefficients, matrices, precision=lax.Precision.HIGHEST)


def apply_adjoint(fields, matrices):
    return jnp.einsum("nrj,nkj->nrk", fields, matrices, precision=lax.Precision.HIGHEST)


def swap_siblings(values):
    return values.reshape((-1, 2) + values.shape[1:])[:, ::-1].reshape(values.shape)


def reference(rhs, leaf_basis, near_tiles, near_pairs, local_transfer, local_coupling, upper_transfer, upper_coupling):
    blocks = rhs.reshape(RHS, LEAVES, LEAF_SIZE)
    basis_wide = leaf_basis.astype(jnp.float32)
    coefficients = jnp.einsum("rni,nik->nrk", blocks.astype(jnp.float32), basis_wide, precision=lax.Precision.HIGHEST)
    trans_local = local_transfer.astype(jnp.float32).reshape(N_LEAF, 2 * LEAF_DEV - 2, RANK, RANK)
    coup_local = local_coupling.astype(jnp.float32).reshape(N_LEAF, 2 * LEAF_DEV - 2, RANK, RANK)
    trans_upper = upper_transfer.astype(jnp.float32)
    coup_upper = upper_coupling.astype(jnp.float32)
    transfers = []
    couplings = []
    for height in range(LOCAL_LEVELS):
        offset = 2 * LEAF_DEV - (2 * LEAF_DEV >> height)
        span = LEAF_DEV >> height
        transfers.append(trans_local[:, offset:offset + span].reshape(N_LEAF * span, RANK, RANK))
        couplings.append(coup_local[:, offset:offset + span].reshape(N_LEAF * span, RANK, RANK))
    for height in range(UP_LEVELS):
        offset = 2 * N_LEAF - (2 * N_LEAF >> height)
        span = N_LEAF >> height
        if height + 1 < UP_LEVELS:
            transfers.append(trans_upper[offset:offset + span])
        couplings.append(coup_upper[offset:offset + span])
    total_levels = LOCAL_LEVELS + UP_LEVELS
    current = coefficients
    far_fields = []
    for height in range(total_levels):
        far_fields.append(apply_transfer(swap_siblings(current), couplings[height]))
        if height + 1 < total_levels:
            carried = apply_transfer(current, transfers[height])
            current = carried[0::2] + carried[1::2]
    fields = far_fields[-1]
    for height in range(total_levels - 2, -1, -1):
        parent = jnp.repeat(fields, 2, axis=0)
        fields = far_fields[height] + apply_adjoint(parent, transfers[height])
    far_out = jnp.einsum("nrk,nik->rni", fields, basis_wide, precision=lax.Precision.HIGHEST)

    pairs_grouped = near_pairs.reshape(N_LEAF, LEAF_DEV, NEAR_PER)
    tiles_grouped = near_tiles.reshape(N_LEAF, LEAF_DEV, NEAR_PER, LEAF_SIZE, LEAF_SIZE)

    def one_group(operands):
        tiles_here, pairs_here = operands
        sources = blocks[:, pairs_here].astype(jnp.float32)
        return jnp.einsum("lpij,rlpj->rli", tiles_here.astype(jnp.float32), sources, precision=lax.Precision.HIGHEST)

    nearby = lax.map(one_group, (tiles_grouped, pairs_grouped))
    nearby = jnp.transpose(nearby, (1, 0, 2, 3)).reshape(RHS, LEAVES, LEAF_SIZE)
    return (far_out + nearby).reshape(RHS, UNKNOWNS)
```

```python
import functools

import jax
import jax.numpy as jnp
from jax import lax
from jax.experimental import pallas as pl
from jax.experimental.pallas import tpu as pltpu
from jax.sharding import PartitionSpec as P

F32 = jnp.float32
BF16 = jnp.bfloat16
ANY = pl.BlockSpec(memory_space=pl.ANY)
VMEM = pl.BlockSpec(memory_space=pltpu.VMEM)
SMEM = pl.BlockSpec(memory_space=pltpu.SMEM)
NEAR_CHUNKS = (4, 6, 6, 6, 6, 4)
LEAVES_PER_STEP = 2


def split_rows(value):
    high = value.astype(BF16)
    low = (value - high.astype(F32)).astype(BF16)
    return jnp.concatenate([high, low], axis=0)


def join_rows(value):
    half = value.shape[0] // 2
    return value[:half] + value[half:]


def times(value, matrix):
    return join_rows(jnp.dot(split_rows(value), matrix, preferred_element_type=F32))


def times_transposed(value, matrix):
    dims = (((1,), (1,)), ((), ()))
    return join_rows(
        lax.dot_general(split_rows(value), matrix, dims, preferred_element_type=F32)
    )


def left_half(shape):
    return lax.broadcasted_iota(jnp.int32, shape, 1) < 64


def apart(pair):
    left = left_half(pair.shape)
    return jnp.concatenate([jnp.where(left, pair, 0.0), jnp.where(left, 0.0, pair)], axis=0)


def pick_nodes(position, matrices, picked):
    nodes = matrices.shape[2]
    count = 2 * 128
    row = lax.broadcasted_iota(jnp.int32, (8, nodes), 0)
    lane = lax.broadcasted_iota(jnp.int32, (8, nodes), 1)
    start = count - lax.shift_right_logical(jnp.full_like(row, count), row)
    wanted = start + lax.shift_right_logical(jnp.full_like(row, position), row)
    chosen = jnp.where(lane == wanted, 1.0, 0.0).astype(BF16)
    dims = (((1,), (1,)), ((), ()))
    for group in range(16):
        block = matrices[4 * group : 4 * group + 4].reshape(256, nodes)
        rows = lax.dot_general(chosen, block, dims, preferred_element_type=F32)
        shifted = pltpu.roll(rows, 64, 1)
        for half in range(2):
            lanes = slice(128 * half, 128 * half + 128)
            picked[pl.ds(4 * group + 2 * half, 8, stride=64), :] = rows[:, lanes]
            other = slice(128 * (1 - half), 128 * (1 - half) + 128)
            del other
            place = (128 * (half + 1)) % 256
            picked[pl.ds(4 * group + 2 * half + 1, 8, stride=64), :] = shifted[:, place : place + 128]


def up_kernel(pos_ref, rhs_hbm, basis_hbm, trans_hbm, upper_hbm, coef_ref, path_ref, upper_ref,
              rhs, basis, trans, upper, picked, sems):
    copies = [
        pltpu.make_async_copy(source, target, sems.at[i])
        for i, (source, target) in enumerate(
            [(rhs_hbm, rhs), (basis_hbm, basis), (trans_hbm, trans), (upper_hbm, upper)]
        )
    ]
    for copy in copies:
        copy.start()
    copies[0].wait()
    copies[1].wait()
    dims = (((1,), (1,)), ((), ()))
    current = []
    for pair in range(16):
        first = rhs[:, 512 * pair : 512 * pair + 256]
        second = rhs[:, 512 * pair + 256 : 512 * pair + 512]
        sources = jnp.concatenate([first, second], axis=0)
        both = lax.dot_general(
            sources, basis[2 * pair : 2 * pair + 2].reshape(128, 256), dims, preferred_element_type=F32
        )
        value = jnp.where(left_half((16, 128)), both[:16], both[16:])
        coef_ref[pair] = value
        current.append(value)
    copies[2].wait()
    base = 0
    while True:
        parents = [
            times(value, trans[2 * (base + i) : 2 * (base + i) + 2].reshape(128, 64))
            for i, value in enumerate(current)
        ]
        base += len(current)
        if len(parents) == 1:
            break
        current = [
            jnp.concatenate([parents[2 * i], parents[2 * i + 1]], axis=1) for i in range(len(parents) // 2)
        ]
        for i, value in enumerate(current):
            coef_ref[base + i] = value
    copies[3].wait()
    pick_nodes(pos_ref[0], upper, picked)
    value = parents[0]
    path_ref[:, 384:448] = value
    for level in range(6):
        matrix = picked[64 * level : 64 * level + 64, 0:64].astype(BF16)
        upper_ref[level] = matrix
        value = times(value, matrix)
        start = 64 * (5 - level)
        path_ref[:, start : start + 64] = value


def up_sweep(position, rhs, basis_t, local_transfer, upper_transfer_t):
    return pl.pallas_call(
        up_kernel,
        out_shape=(
            jax.ShapeDtypeStruct((31, 16, 128), F32),
            jax.ShapeDtypeStruct((16, 448), F32),
            jax.ShapeDtypeStruct((6, 64, 64), BF16),
        ),
        in_specs=[SMEM, ANY, ANY, ANY, ANY],
        out_specs=(VMEM, VMEM, VMEM),
        scratch_shapes=[
            pltpu.VMEM(rhs.shape, BF16),
            pltpu.VMEM(basis_t.shape, BF16),
            pltpu.VMEM(local_transfer.shape, BF16),
            pltpu.VMEM(upper_transfer_t.shape, BF16),
            pltpu.VMEM((512, 128), F32),
            pltpu.SemaphoreType.DMA((4,)),
        ],
        compiler_params=pltpu.CompilerParams(vmem_limit_bytes=20 * 2**20),
        cost_estimate=pl.CostEstimate(flops=10**8, bytes_accessed=5 * 2**20, transcendentals=0),
        name="up_sweep",
    )(position, rhs, basis_t, local_transfer, upper_transfer_t)


def far_kernel(pos_ref, coef, coup_hbm, upper_hbm, far_ref, upper_ref, coup, upper, picked, sems):
    copies = [
        pltpu.make_async_copy(coup_hbm, coup, sems.at[0]),
        pltpu.make_async_copy(upper_hbm, upper, sems.at[1]),
    ]
    for copy in copies:
        copy.start()
    copies[0].wait()
    for pair in range(31):
        swapped = pltpu.roll(coef[pair], 64, 1)
        both = times(apart(swapped), coup[2 * pair : 2 * pair + 2].reshape(128, 64))
        far_ref[pair] = jnp.concatenate([both[:16], both[16:]], axis=1)
    copies[1].wait()
    pick_nodes(pos_ref[0], upper, picked)
    for level in range(7):
        upper_ref[level] = picked[64 * level : 64 * level + 64, 0:64].astype(BF16)


def far_fields(position, coef, local_coupling, upper_coupling_t):
    return pl.pallas_call(
        far_kernel,
        out_shape=(
            jax.ShapeDtypeStruct((31, 16, 128), F32),
            jax.ShapeDtypeStruct((7, 64, 64), BF16),
        ),
        in_specs=[SMEM, VMEM, ANY, ANY],
        out_specs=(VMEM, VMEM),
        scratch_shapes=[
            pltpu.VMEM(local_coupling.shape, BF16),
            pltpu.VMEM(upper_coupling_t.shape, BF16),
            pltpu.VMEM((512, 128), F32),
            pltpu.SemaphoreType.DMA((2,)),
        ],
        compiler_params=pltpu.CompilerParams(vmem_limit_bytes=20 * 2**20),
        cost_estimate=pl.CostEstimate(flops=10**8, bytes_accessed=5 * 2**20, transcendentals=0),
        name="far_fields",
    )(position, coef, local_coupling, upper_coupling_t)


def near_kernel(first, index_ref, before, own, after, order, tiles, out_ref):
    del order
    step = pl.program_id(0)
    dims = (((1,), (1,)), ((), ()))
    for i in range(LEAVES_PER_STEP):
        leaf = first + step * LEAVES_PER_STEP + i
        total = jnp.zeros((16, 256), F32)
        for k in range(4):
            index = index_ref[leaf, k]
            side = lax.shift_right_logical(index, 5)
            column = pl.ds(pl.multiple_of((index & 31) * 256, 256), 256)
            source = jnp.where(
                side == 0, before[:, column], jnp.where(side == 1, own[:, column], after[:, column])
            )
            total += lax.dot_general(source, tiles[i, k], dims, preferred_element_type=F32)
        out_ref[:, 256 * i : 256 * i + 256] = total


def near_field(first, count, index, before, own, after, order, tiles):
    steps = count // LEAVES_PER_STEP
    start = first // LEAVES_PER_STEP
    return pl.pallas_call(
        functools.partial(near_kernel, first),
        grid=(steps,),
        out_shape=jax.ShapeDtypeStruct((16, 256 * count), F32),
        in_specs=[
            SMEM,
            VMEM,
            VMEM,
            VMEM,
            ANY,
            pl.BlockSpec((LEAVES_PER_STEP, 4, 256, 256), lambda i: (start + i, 0, 0, 0)),
        ],
        out_specs=pl.BlockSpec((16, 256 * LEAVES_PER_STEP), lambda i: (0, i)),
        compiler_params=pltpu.CompilerParams(vmem_limit_bytes=20 * 2**20),
        cost_estimate=pl.CostEstimate(
            flops=count * 4 * 256 * 256 * 32, bytes_accessed=count * 4 * 2**17, transcendentals=0
        ),
        name="near_field",
    )(index, before, own, after, order, tiles)


def down_kernel(*refs):
    siblings = refs[:7]
    upper_trans, upper_coup, far, trans_hbm, basis_hbm = refs[7:12]
    nearby = refs[12 : 12 + len(NEAR_CHUNKS)]
    out_ref, trans, basis, sems = refs[12 + len(NEAR_CHUNKS) :]
    copies = [
        pltpu.make_async_copy(trans_hbm, trans, sems.at[0]),
        pltpu.make_async_copy(basis_hbm, basis, sems.at[1]),
    ]
    for copy in copies:
        copy.start()
    field = None
    for level in range(6, -1, -1):
        width = 64 * (7 - level)
        term = times(siblings[level][:, width - 64 : width], upper_coup[level])
        field = term if field is None else term + times_transposed(field, upper_trans[level])
    copies[0].wait()
    fields = [field]
    base = 31
    while len(fields) < 32:
        base -= len(fields)
        pairs = [
            far[base + i] + times_transposed(value, trans[2 * (base + i) : 2 * (base + i) + 2].reshape(128, 64))
            for i, value in enumerate(fields)
        ]
        if len(pairs) == 16:
            break
        fields = []
        for pair in pairs:
            fields += [pair[:, 0:64], pair[:, 64:128]]
    copies[1].wait()
    leaf = 0
    for nearby_ref, count in zip(nearby, NEAR_CHUNKS):
        for i in range(0, count, 2):
            both = times(apart(pairs[leaf // 2]), basis[leaf : leaf + 2].reshape(128, 256))
            for j in range(2):
                out_ref[:, 256 * (leaf + j) : 256 * (leaf + j) + 256] = (
                    both[16 * j : 16 * j + 16] + nearby_ref[:, 256 * (i + j) : 256 * (i + j) + 256]
                )
            leaf += 2


def down_sweep(siblings, upper_trans, upper_coup, far, local_transfer, basis_t, nearby):
    return pl.pallas_call(
        down_kernel,
        out_shape=jax.ShapeDtypeStruct((16, 8192), F32),
        in_specs=[VMEM] * 10 + [ANY, ANY] + [VMEM] * len(nearby),
        out_specs=VMEM,
        scratch_shapes=[
            pltpu.VMEM(local_transfer.shape, BF16),
            pltpu.VMEM(basis_t.shape, BF16),
            pltpu.SemaphoreType.DMA((2,)),
        ],
        compiler_params=pltpu.CompilerParams(vmem_limit_bytes=20 * 2**20),
        cost_estimate=pl.CostEstimate(flops=10**8, bytes_accessed=5 * 2**20, transcendentals=0),
        name="down_sweep",
    )(*siblings, upper_trans, upper_coup, far, local_transfer, basis_t, *nearby)


def local(rhs, leaf_basis, near_tiles, near_pairs, local_transfer, local_coupling, upper_transfer, upper_coupling):
    devices = lax.axis_size("leaf")
    position = lax.axis_index("leaf").astype(jnp.int32)
    up = [(i, i + 1) for i in range(devices - 1)]
    before = lax.ppermute(rhs, "leaf", up)
    after = lax.ppermute(rhs, "leaf", [(j, i) for i, j in up])
    index = near_pairs - (position * 32 - 32)
    basis_t = jnp.transpose(leaf_basis, (0, 2, 1))
    where = position.reshape(1)
    coef, path, upper_trans = up_sweep(
        where, rhs, basis_t, local_transfer, jnp.transpose(upper_transfer, (1, 2, 0))
    )
    nearby = []
    siblings = []
    first = 0
    for level in range(7):
        width = 64 * (7 - level)
        pairs = [(i, i ^ (1 << level)) for i in range(devices)]
        received = lax.ppermute(path, "leaf", pairs)
        if level == 0:
            far, upper_coup = far_fields(where, coef, local_coupling, jnp.transpose(upper_coupling, (1, 2, 0)))
            received, far = lax.optimization_barrier((received, far))
        else:
            count = NEAR_CHUNKS[level - 1]
            part = near_field(first, count, index, before, rhs, after, path, near_tiles)
            first += count
            received, part = lax.optimization_barrier((received, part))
            nearby.append(part)
        siblings.append(received)
        path = path[:, : width - 64] + received[:, : width - 64]
    return down_sweep(siblings, upper_trans, upper_coup, far, local_transfer, basis_t, nearby)


def solution(mesh):
    return jax.shard_map(
        local,
        mesh=mesh,
        in_specs=(
            P(None, "leaf"),
            P("leaf", None, None),
            P("leaf", None, None, None),
            P("leaf", None),
            P("leaf", None, None),
            P("leaf", None, None),
            P(),
            P(),
        ),
        out_specs=P(None, "leaf"),
        check_vma=False,
    )
```

```python
import functools

import jax
import jax.numpy as jnp
from jax import lax
from jax.experimental import pallas as pl
from jax.experimental.pallas import tpu as pltpu
from jax.sharding import PartitionSpec as P

F32 = jnp.float32
BF16 = jnp.bfloat16
ANY = pl.BlockSpec(memory_space=pl.ANY)
VMEM = pl.BlockSpec(memory_space=pltpu.VMEM)
HBM = pl.BlockSpec(memory_space=pltpu.HBM)
SMEM = pl.BlockSpec(memory_space=pltpu.SMEM)
NEAR_CHUNKS = (6, 6, 6, 6, 6, 2)
FETCH = (8, 4, 6, 7, 7)
MASKS = (1, 2, 6, 8, 24, 32, 96)


def split_rows(value):
    high = value.astype(BF16)
    low = (value - high.astype(F32)).astype(BF16)
    return jnp.concatenate([high, low], axis=0)


def join_rows(value):
    half = value.shape[0] // 2
    return value[:half] + value[half:]


def times(value, matrix):
    return join_rows(jnp.dot(split_rows(value), matrix, preferred_element_type=F32))


def times_transposed(value, matrix):
    dims = (((1,), (1,)), ((), ()))
    return join_rows(
        lax.dot_general(split_rows(value), matrix, dims, preferred_element_type=F32)
    )


def left_half(shape):
    return lax.broadcasted_iota(jnp.int32, shape, 1) < 64


def apart(pair):
    left = left_half(pair.shape)
    return jnp.concatenate([jnp.where(left, pair, 0.0), jnp.where(left, 0.0, pair)], axis=0)


def pick_nodes(position, matrices, picked):
    nodes = matrices.shape[2]
    count = 2 * 128
    row = lax.broadcasted_iota(jnp.int32, (8, nodes), 0)
    lane = lax.broadcasted_iota(jnp.int32, (8, nodes), 1)
    start = count - lax.shift_right_logical(jnp.full_like(row, count), row)
    wanted = start + lax.shift_right_logical(jnp.full_like(row, position), row)
    chosen = jnp.where(lane == wanted, 1.0, 0.0).astype(BF16)
    dims = (((1,), (1,)), ((), ()))
    for group in range(16):
        block = matrices[4 * group : 4 * group + 4].reshape(256, nodes)
        rows = lax.dot_general(chosen, block, dims, preferred_element_type=F32)
        shifted = pltpu.roll(rows, 64, 1)
        for half in range(2):
            lanes = slice(128 * half, 128 * half + 128)
            picked[pl.ds(4 * group + 2 * half, 8, stride=64), :] = rows[:, lanes]
            other = slice(128 * (1 - half), 128 * (1 - half) + 128)
            del other
            place = (128 * (half + 1)) % 256
            picked[pl.ds(4 * group + 2 * half + 1, 8, stride=64), :] = shifted[:, place : place + 128]


def in_hbm(*arrays):
    return [pltpu.with_memory_space_constraint(array, pltpu.HBM) for array in arrays]


def vmem(shape, dtype):
    return pltpu.VMEM(shape, dtype)


def vmem_like(array):
    return vmem(array.shape, array.dtype)


def tiles_like(tiles, count):
    return vmem((count,) + tiles.shape[1:], tiles.dtype)


def start_all(pairs, sems):
    copies = [pltpu.make_async_copy(source, target, sems.at[i]) for i, (source, target) in enumerate(pairs)]
    for copy in copies:
        copy.start()
    return copies


def params():
    return pltpu.CompilerParams(vmem_limit_bytes=24 * 2**20)


def cost(flops, size):
    return pl.CostEstimate(flops=flops, bytes_accessed=size, transcendentals=0)


def up_kernel(pos_ref, rhs_hbm, basis_hbm, trans_hbm, upper_hbm, upper_coup_hbm, coup_hbm, tiles_hbm,
              coef_ref, path_ref, upper_ref, rhs, basis, trans, upper_coup, coup, tiles,
              upper, picked, sems):
    copies = start_all(
        [
            (rhs_hbm, rhs),
            (basis_hbm, basis),
            (trans_hbm, trans),
            (upper_hbm, upper),
            (upper_coup_hbm, upper_coup),
            (tiles_hbm.at[: FETCH[0]], tiles),
            (coup_hbm, coup),
        ],
        sems,
    )
    copies[0].wait()
    copies[1].wait()
    dims = (((1,), (1,)), ((), ()))
    current = []
    for pair in range(16):
        first = rhs[:, 512 * pair : 512 * pair + 256]
        second = rhs[:, 512 * pair + 256 : 512 * pair + 512]
        sources = jnp.concatenate([first, second], axis=0)
        both = lax.dot_general(
            sources, basis[2 * pair : 2 * pair + 2].reshape(128, 256), dims, preferred_element_type=F32
        )
        value = jnp.where(left_half((16, 128)), both[:16], both[16:])
        coef_ref[pair] = value
        current.append(value)
    copies[2].wait()
    base = 0
    while True:
        parents = [
            times(value, trans[2 * (base + i) : 2 * (base + i) + 2].reshape(128, 64))
            for i, value in enumerate(current)
        ]
        base += len(current)
        if len(parents) == 1:
            break
        current = [
            jnp.concatenate([parents[2 * i], parents[2 * i + 1]], axis=1) for i in range(len(parents) // 2)
        ]
        for i, value in enumerate(current):
            coef_ref[base + i] = value
    copies[3].wait()
    pick_nodes(pos_ref[0], upper, picked)
    value = parents[0]
    path_ref[:, 384:448] = value
    for level in range(6):
        matrix = picked[64 * level : 64 * level + 64, 0:64].astype(BF16)
        upper_ref[level] = matrix
        value = times(value, matrix)
        start = 64 * (5 - level)
        path_ref[:, start : start + 64] = value
    for copy in copies[4:]:
        copy.wait()


def up_sweep(position, rhs, basis_t, local_transfer, upper_transfer_t, upper_coupling_t, local_coupling, tiles):
    return pl.pallas_call(
        up_kernel,
        out_shape=(
            vmem((31, 16, 128), F32),
            vmem((16, 448), F32),
            vmem((6, 64, 64), BF16),
            vmem_like(rhs),
            vmem_like(basis_t),
            vmem_like(local_transfer),
            vmem_like(upper_coupling_t),
            vmem_like(local_coupling),
            tiles_like(tiles, FETCH[0]),
        ),
        in_specs=[SMEM] + [HBM] * 7,
        out_specs=(VMEM,) * 9,
        scratch_shapes=[
            pltpu.VMEM(upper_transfer_t.shape, BF16),
            pltpu.VMEM((512, 128), F32),
            pltpu.SemaphoreType.DMA((7,)),
        ],
        compiler_params=params(),
        cost_estimate=cost(4 * 10**9, 12 * 2**20),
        name="up_sweep",
    )(
        position,
        *in_hbm(rhs, basis_t, local_transfer, upper_transfer_t, upper_coupling_t, local_coupling, tiles),
    )


def pick_kernel(pos_ref, order, upper, tiles_hbm, *refs):
    del order
    upper_ref, tiles, picked, sems = refs[-4:]
    copies = start_all([(tiles_hbm.at[FETCH[0] : FETCH[0] + FETCH[1]], tiles)], sems)
    pick_nodes(pos_ref[0], upper, picked)
    for level in range(7):
        upper_ref[level] = picked[64 * level : 64 * level + 64, 0:64].astype(BF16)
    copies[0].wait()


def pick_couplings(position, order, upper_coupling_t, tiles, keep):
    return pl.pallas_call(
        pick_kernel,
        out_shape=(vmem((7, 64, 64), BF16), tiles_like(tiles, FETCH[1])),
        in_specs=[SMEM, ANY, VMEM, HBM] + [VMEM] * len(keep),
        out_specs=(VMEM, VMEM),
        scratch_shapes=[pltpu.VMEM((512, 128), F32), pltpu.SemaphoreType.DMA((1,))],
        compiler_params=params(),
        cost_estimate=cost(10**9, 2**20),
        name="pick_couplings",
    )(position, order, upper_coupling_t, *in_hbm(tiles), *keep)


def near_kernel(first, count, fetched, fetch, with_far, *refs):
    pos_ref, pairs_ref, order, inner, own, outer = refs[:6]
    del order
    at = 6
    held = refs[at : at + fetched]
    at += fetched
    coef, coup = refs[at : at + 2]
    at += 4
    if fetch:
        tiles_hbm = refs[at]
        at += 1
    out_ref = refs[at]
    at += 1
    if with_far:
        far_ref = refs[at]
        at += 1
    if fetch:
        start = sum(FETCH[:fetch])
        copies = start_all([(tiles_hbm.at[start : start + FETCH[fetch]], refs[at])], refs[at + 1])
    dims = (((1,), (1,)), ((), ()))
    position = pos_ref[0]
    for i in range(count):
        total = None
        place = first + i
        box = 0
        while place >= FETCH[box]:
            place -= FETCH[box]
            box += 1
        for k in range(4):
            leaf = pairs_ref[k, first + i]
            holder = lax.shift_right_logical(leaf, 5)
            column = pl.ds(pl.multiple_of((leaf & 31) * 256, 256), 256)
            source = jnp.where(
                holder == position, own[:, column],
                jnp.where(holder == position ^ 1, inner[:, column], outer[:, column]),
            )
            part = lax.dot_general(source, held[box][place, k], dims, preferred_element_type=F32)
            total = part if total is None else total + part
        out_ref[:, 256 * i : 256 * i + 256] = total
    if with_far:
        for pair in range(31):
            swapped = pltpu.roll(coef[pair], 64, 1)
            both = times(apart(swapped), coup[2 * pair : 2 * pair + 2].reshape(128, 64))
            far_ref[pair] = jnp.concatenate([both[:16], both[16:]], axis=1)
    if fetch:
        copies[0].wait()


def near_field(first, count, position, near_pairs_t, order, inner, own, outer, held, keep, fetch, tiles, with_far):
    inputs = [position, near_pairs_t, order, inner, own, outer, *held, *keep]
    in_specs = [SMEM, SMEM, ANY] + [VMEM] * (len(inputs) - 3)
    outputs = [vmem((16, 256 * count), F32)]
    scratch = []
    if with_far:
        outputs.append(vmem((31, 16, 128), F32))
    if fetch:
        inputs += in_hbm(tiles)
        in_specs.append(HBM)
        outputs.append(tiles_like(tiles, FETCH[fetch]))
        scratch = [pltpu.SemaphoreType.DMA((1,))]
    return pl.pallas_call(
        functools.partial(near_kernel, first, count, len(held), fetch, with_far),
        out_shape=tuple(outputs),
        in_specs=in_specs,
        out_specs=(VMEM,) * len(outputs),
        scratch_shapes=scratch,
        compiler_params=params(),
        cost_estimate=cost(10**9, 2**20),
        name="near_field",
    )(*inputs)


def down_kernel(*refs):
    siblings = refs[:7]
    upper_trans, upper_coup, far, trans, basis = refs[7:12]
    nearby = refs[12 : 12 + len(NEAR_CHUNKS)]
    out_ref = refs[12 + len(NEAR_CHUNKS)]
    field = None
    for level in range(6, -1, -1):
        width = 64 * (7 - level)
        term = times(siblings[level][:, width - 64 : width], upper_coup[level])
        field = term if field is None else term + times_transposed(field, upper_trans[level])
    fields = [field]
    base = 31
    while len(fields) < 32:
        base -= len(fields)
        pairs = [
            far[base + i] + times_transposed(value, trans[2 * (base + i) : 2 * (base + i) + 2].reshape(128, 64))
            for i, value in enumerate(fields)
        ]
        if len(pairs) == 16:
            break
        fields = []
        for pair in pairs:
            fields += [pair[:, 0:64], pair[:, 64:128]]
    leaf = 0
    for nearby_ref, count in zip(nearby, NEAR_CHUNKS):
        for i in range(0, count, 2):
            both = times(apart(pairs[leaf // 2]), basis[leaf : leaf + 2].reshape(128, 256))
            for j in range(2):
                out_ref[:, 256 * (leaf + j) : 256 * (leaf + j) + 256] = (
                    both[16 * j : 16 * j + 16] + nearby_ref[:, 256 * (i + j) : 256 * (i + j) + 256]
                )
            leaf += 2


def down_sweep(siblings, upper_trans, upper_coup, far, local_transfer, basis_t, nearby):
    return pl.pallas_call(
        down_kernel,
        out_shape=jax.ShapeDtypeStruct((16, 8192), F32),
        in_specs=[VMEM] * (12 + len(nearby)),
        out_specs=VMEM,
        compiler_params=params(),
        cost_estimate=cost(3 * 10**9, 2**20),
        name="down_sweep",
    )(*siblings, upper_trans, upper_coup, far, local_transfer, basis_t, *nearby)


def local(rhs, leaf_basis, near_tiles, near_pairs, local_transfer, local_coupling, upper_transfer, upper_coupling):
    devices = lax.axis_size("leaf")
    position = lax.axis_index("leaf").astype(jnp.int32)
    last = devices - 1
    outward = [(i, min(max(i + 2 * (i & 1) - 1, 0), last)) for i in range(devices)]
    outer = lax.ppermute(rhs, "leaf", outward)
    inner = lax.ppermute(rhs, "leaf", [(i, i ^ 1) for i in range(devices)])
    near_pairs_t = jnp.transpose(near_pairs, (1, 0))
    basis_t = jnp.transpose(leaf_basis, (0, 2, 1))
    where = position.reshape(1)
    coef, path, upper_trans, own, basis, trans, upper_coup, coup, tiles = up_sweep(
        where,
        rhs,
        basis_t,
        local_transfer,
        jnp.transpose(upper_transfer, (1, 2, 0)),
        jnp.transpose(upper_coupling, (1, 2, 0)),
        local_coupling,
        near_tiles,
    )
    held = [tiles]
    keep = [coef, coup, trans, basis]
    nearby = []
    siblings = []
    first = 0
    for level in range(7):
        width = 64 * (7 - level)
        pairs = [(i, i ^ MASKS[level]) for i in range(devices)]
        received = lax.ppermute(path, "leaf", pairs)
        if level == 0:
            upper_coup, tiles = pick_couplings(where, path, upper_coup, near_tiles, held + keep)
            held.append(tiles)
            received, upper_coup = lax.optimization_barrier((received, upper_coup))
        else:
            count = NEAR_CHUNKS[level - 1]
            fetch = level + 1 if level + 1 < len(FETCH) else 0
            last_chunk = level == 6
            results = near_field(
                first, count, where, near_pairs_t, path, inner, own, outer, held, keep, fetch, near_tiles, last_chunk
            )
            part = results[0]
            if fetch:
                held.append(results[-1])
            if last_chunk:
                far = results[1]
            first += count
            received, part = lax.optimization_barrier((received, part))
            nearby.append(part)
        siblings.append(received)
        path = path[:, : width - 64] + received[:, : width - 64]
    return down_sweep(siblings, upper_trans, upper_coup, far, trans, basis, nearby)


def solution(mesh):
    return jax.shard_map(
        local,
        mesh=mesh,
        in_specs=(
            P(None, "leaf"),
            P("leaf", None, None),
            P("leaf", None, None, None),
            P("leaf", None),
            P("leaf", None, None),
            P("leaf", None, None),
            P(),
            P(),
        ),
        out_specs=P(None, "leaf"),
        check_vma=False,
    )
```

```python
import functools

import jax
import jax.numpy as jnp
from jax import lax
from jax.experimental import pallas as pl
from jax.experimental.pallas import tpu as pltpu
from jax.sharding import PartitionSpec as P

F32 = jnp.float32
BF16 = jnp.bfloat16
ANY = pl.BlockSpec(memory_space=pl.ANY)
VMEM = pl.BlockSpec(memory_space=pltpu.VMEM)
HBM = pl.BlockSpec(memory_space=pltpu.HBM)
SMEM = pl.BlockSpec(memory_space=pltpu.SMEM)
NEAR_CHUNKS = (6, 6, 6, 7, 7)
MASKS = (1, 3, 7, 9, 25, 33, 97)


def split_rows(value):
    high = value.astype(BF16)
    low = (value - high.astype(F32)).astype(BF16)
    return jnp.concatenate([high, low], axis=0)


def join_rows(value):
    half = value.shape[0] // 2
    return value[:half] + value[half:]


def times(value, matrix):
    return join_rows(jnp.dot(split_rows(value), matrix, preferred_element_type=F32))


def times_transposed(value, matrix):
    dims = (((1,), (1,)), ((), ()))
    return join_rows(
        lax.dot_general(split_rows(value), matrix, dims, preferred_element_type=F32)
    )


def left_half(shape):
    return lax.broadcasted_iota(jnp.int32, shape, 1) < 64


def apart(pair):
    left = left_half(pair.shape)
    return jnp.concatenate([jnp.where(left, pair, 0.0), jnp.where(left, 0.0, pair)], axis=0)


def pick_nodes(position, matrices, picked):
    nodes = matrices.shape[2]
    count = 2 * 128
    row = lax.broadcasted_iota(jnp.int32, (8, nodes), 0)
    lane = lax.broadcasted_iota(jnp.int32, (8, nodes), 1)
    start = count - lax.shift_right_logical(jnp.full_like(row, count), row)
    wanted = start + lax.shift_right_logical(jnp.full_like(row, position), row)
    chosen = jnp.where(lane == wanted, 1.0, 0.0).astype(BF16)
    dims = (((1,), (1,)), ((), ()))
    for group in range(16):
        block = matrices[4 * group : 4 * group + 4].reshape(256, nodes)
        rows = lax.dot_general(chosen, block, dims, preferred_element_type=F32)
        shifted = pltpu.roll(rows, 64, 1)
        for half in range(2):
            lanes = slice(128 * half, 128 * half + 128)
            picked[pl.ds(4 * group + 2 * half, 8, stride=64), :] = rows[:, lanes]
            other = slice(128 * (1 - half), 128 * (1 - half) + 128)
            del other
            place = (128 * (half + 1)) % 256
            picked[pl.ds(4 * group + 2 * half + 1, 8, stride=64), :] = shifted[:, place : place + 128]


def in_hbm(*arrays):
    return [pltpu.with_memory_space_constraint(array, pltpu.HBM) for array in arrays]


def vmem(shape, dtype):
    return pltpu.VMEM(shape, dtype)


def vmem_like(array):
    return vmem(array.shape, array.dtype)


def tiles_like(tiles, count):
    return vmem((count,) + tiles.shape[1:], tiles.dtype)


def start_all(pairs, sems):
    copies = [pltpu.make_async_copy(source, target, sems.at[i]) for i, (source, target) in enumerate(pairs)]
    for copy in copies:
        copy.start()
    return copies


def params():
    return pltpu.CompilerParams(vmem_limit_bytes=24 * 2**20)


def cost(flops, size):
    return pl.CostEstimate(flops=flops, bytes_accessed=size, transcendentals=0)


def up_kernel(pos_ref, rhs_hbm, basis_hbm, trans_hbm, upper_hbm, upper_coup_hbm, coup_hbm,
              coef_ref, path_ref, upper_ref, rhs, basis, trans, upper_coup, coup,
              upper, picked, sems):
    copies = start_all(
        [
            (rhs_hbm, rhs),
            (basis_hbm, basis),
            (trans_hbm, trans),
            (upper_hbm, upper),
            (upper_coup_hbm, upper_coup),
            (coup_hbm, coup),
        ],
        sems,
    )
    copies[0].wait()
    copies[1].wait()
    dims = (((1,), (1,)), ((), ()))
    current = []
    for pair in range(16):
        first = rhs[:, 512 * pair : 512 * pair + 256]
        second = rhs[:, 512 * pair + 256 : 512 * pair + 512]
        sources = jnp.concatenate([first, second], axis=0)
        both = lax.dot_general(
            sources, basis[2 * pair : 2 * pair + 2].reshape(128, 256), dims, preferred_element_type=F32
        )
        value = jnp.where(left_half((16, 128)), both[:16], both[16:])
        coef_ref[pair] = value
        current.append(value)
    copies[2].wait()
    base = 0
    while True:
        parents = [
            times(value, trans[2 * (base + i) : 2 * (base + i) + 2].reshape(128, 64))
            for i, value in enumerate(current)
        ]
        base += len(current)
        if len(parents) == 1:
            break
        current = [
            jnp.concatenate([parents[2 * i], parents[2 * i + 1]], axis=1) for i in range(len(parents) // 2)
        ]
        for i, value in enumerate(current):
            coef_ref[base + i] = value
    copies[3].wait()
    pick_nodes(pos_ref[0], upper, picked)
    value = parents[0]
    path_ref[:, 384:448] = value
    for level in range(6):
        matrix = picked[64 * level : 64 * level + 64, 0:64].astype(BF16)
        upper_ref[level] = matrix
        value = times(value, matrix)
        start = 64 * (5 - level)
        path_ref[:, start : start + 64] = value
    for copy in copies[4:]:
        copy.wait()


def up_sweep(position, rhs, basis_t, local_transfer, upper_transfer_t, upper_coupling_t, local_coupling):
    return pl.pallas_call(
        up_kernel,
        out_shape=(
            vmem((31, 16, 128), F32),
            vmem((16, 448), F32),
            vmem((6, 64, 64), BF16),
            vmem_like(rhs),
            vmem_like(basis_t),
            vmem_like(local_transfer),
            vmem_like(upper_coupling_t),
            vmem_like(local_coupling),
        ),
        in_specs=[SMEM] + [HBM] * 6,
        out_specs=(VMEM,) * 8,
        scratch_shapes=[
            pltpu.VMEM(upper_transfer_t.shape, BF16),
            pltpu.VMEM((512, 128), F32),
            pltpu.SemaphoreType.DMA((6,)),
        ],
        compiler_params=params(),
        cost_estimate=cost(4 * 10**9, 12 * 2**20),
        name="up_sweep",
    )(
        position,
        *in_hbm(rhs, basis_t, local_transfer, upper_transfer_t, upper_coupling_t, local_coupling),
    )


def pick_kernel(pos_ref, order, upper, *refs):
    del order
    upper_ref, picked = refs[-2:]
    pick_nodes(pos_ref[0], upper, picked)
    for level in range(7):
        upper_ref[level] = picked[64 * level : 64 * level + 64, 0:64].astype(BF16)


def pick_couplings(position, order, upper_coupling_t, keep):
    return pl.pallas_call(
        pick_kernel,
        out_shape=vmem((7, 64, 64), BF16),
        in_specs=[SMEM, ANY, VMEM] + [VMEM] * len(keep),
        out_specs=VMEM,
        scratch_shapes=[pltpu.VMEM((512, 128), F32)],
        compiler_params=params(),
        cost_estimate=cost(10**9, 2**20),
        name="pick_couplings",
    )(position, order, upper_coupling_t, *keep)


def far_kernel(order, coef, coup, *refs):
    del order
    far_ref = refs[-1]
    for pair in range(31):
        swapped = pltpu.roll(coef[pair], 64, 1)
        both = times(apart(swapped), coup[2 * pair : 2 * pair + 2].reshape(128, 64))
        far_ref[pair] = jnp.concatenate([both[:16], both[16:]], axis=1)


def far_fields(order, coef, coup, keep):
    return pl.pallas_call(
        far_kernel,
        out_shape=vmem((31, 16, 128), F32),
        in_specs=[ANY] + [VMEM] * (2 + len(keep)),
        out_specs=VMEM,
        compiler_params=params(),
        cost_estimate=cost(10**9, 2**20),
        name="far_fields",
    )(order, coef, coup, *keep)


def near_kernel(first, count, pos_ref, pairs_ref, order, inner, own, outer, tiles, *refs):
    del order
    out_ref = refs[-1]
    dims = (((1,), (1,)), ((), ()))
    position = pos_ref[0]
    for i in range(count):
        total = None
        for k in range(4):
            leaf = pairs_ref[k, first + i]
            holder = lax.shift_right_logical(leaf, 5)
            column = pl.ds(pl.multiple_of((leaf & 31) * 256, 256), 256)
            source = jnp.where(
                holder == position, own[:, column],
                jnp.where(holder == position ^ 1, inner[:, column], outer[:, column]),
            )
            part = lax.dot_general(source, tiles[first + i, k], dims, preferred_element_type=F32)
            total = part if total is None else total + part
        out_ref[:, 256 * i : 256 * i + 256] = total


def near_field(first, count, position, near_pairs_t, order, inner, own, outer, tiles, keep):
    return pl.pallas_call(
        functools.partial(near_kernel, first, count),
        out_shape=vmem((16, 256 * count), F32),
        in_specs=[SMEM, SMEM, ANY] + [VMEM] * (4 + len(keep)),
        out_specs=VMEM,
        compiler_params=params(),
        cost_estimate=cost(10**9, 2**20),
        name="near_field",
    )(position, near_pairs_t, order, inner, own, outer, tiles, *keep)


def down_kernel(*refs):
    siblings = refs[:7]
    upper_trans, upper_coup, far, trans, basis = refs[7:12]
    nearby = refs[12 : 12 + len(NEAR_CHUNKS)]
    out_ref = refs[12 + len(NEAR_CHUNKS)]
    field = None
    for level in range(6, -1, -1):
        width = 64 * (7 - level)
        term = times(siblings[level][:, width - 64 : width], upper_coup[level])
        field = term if field is None else term + times_transposed(field, upper_trans[level])
    fields = [field]
    base = 31
    while len(fields) < 32:
        base -= len(fields)
        pairs = [
            far[base + i] + times_transposed(value, trans[2 * (base + i) : 2 * (base + i) + 2].reshape(128, 64))
            for i, value in enumerate(fields)
        ]
        if len(pairs) == 16:
            break
        fields = []
        for pair in pairs:
            fields += [pair[:, 0:64], pair[:, 64:128]]
    places = [(box, i) for box, count in enumerate(NEAR_CHUNKS) for i in range(count)]
    for leaf in range(0, 32, 2):
        both = times(apart(pairs[leaf // 2]), basis[leaf : leaf + 2].reshape(128, 256))
        for j in range(2):
            box, i = places[leaf + j]
            out_ref[:, 256 * (leaf + j) : 256 * (leaf + j) + 256] = (
                both[16 * j : 16 * j + 16] + nearby[box][:, 256 * i : 256 * i + 256]
            )


def down_sweep(siblings, upper_trans, upper_coup, far, local_transfer, basis_t, nearby):
    return pl.pallas_call(
        down_kernel,
        out_shape=jax.ShapeDtypeStruct((16, 8192), F32),
        in_specs=[VMEM] * (12 + len(nearby)),
        out_specs=VMEM,
        compiler_params=params(),
        cost_estimate=cost(3 * 10**9, 2**20),
        name="down_sweep",
    )(*siblings, upper_trans, upper_coup, far, local_transfer, basis_t, *nearby)


def local(rhs, leaf_basis, near_tiles, near_pairs, local_transfer, local_coupling, upper_transfer, upper_coupling):
    devices = lax.axis_size("leaf")
    position = lax.axis_index("leaf").astype(jnp.int32)
    where = position.reshape(1)
    last = devices - 1
    outward = [(i, min(max(i + 2 * (i & 1) - 1, 0), last)) for i in range(devices)]
    inward = [(i, i ^ 1) for i in range(devices)]
    near_pairs_t = jnp.transpose(near_pairs, (1, 0))
    coef, path, upper_trans, own, basis, trans, upper_coup, coup = up_sweep(
        where,
        rhs,
        jnp.transpose(leaf_basis, (0, 2, 1)),
        local_transfer,
        jnp.transpose(upper_transfer, (1, 2, 0)),
        jnp.transpose(upper_coupling, (1, 2, 0)),
        local_coupling,
    )
    outer = lax.ppermute(own, "leaf", outward)
    inner = lax.ppermute(own, "leaf", inward)
    nearby = []
    siblings = []
    first = 0
    for level in range(7):
        width = 64 * (7 - level)
        pairs = [(i, i ^ MASKS[level]) for i in range(devices)]
        received = lax.ppermute(path, "leaf", pairs)
        if level == 0:
            upper_coup = pick_couplings(where, path, upper_coup, [coef, coup, trans, basis])
            received, upper_coup = lax.optimization_barrier((received, upper_coup))
        elif level == 1:
            far = far_fields(path, coef, coup, [trans, basis])
            received, far = lax.optimization_barrier((received, far))
        else:
            count = NEAR_CHUNKS[level - 2]
            part = near_field(
                first, count, where, near_pairs_t, path, inner, own, outer, near_tiles, [far, trans, basis]
            )
            first += count
            received, part = lax.optimization_barrier((received, part))
            nearby.append(part)
        siblings.append(received)
        path = path[:, : width - 64] + received[:, : width - 64]
    return down_sweep(siblings, upper_trans, upper_coup, far, trans, basis, nearby)


def solution(mesh):
    return jax.shard_map(
        local,
        mesh=mesh,
        in_specs=(
            P(None, "leaf"),
            P("leaf", None, None),
            P("leaf", None, None, None),
            P("leaf", None),
            P("leaf", None, None),
            P("leaf", None, None),
            P(),
            P(),
        ),
        out_specs=P(None, "leaf"),
        check_vma=False,
    )
```

```python
import functools

import jax
import jax.numpy as jnp
from jax import lax
from jax.experimental import pallas as pl
from jax.experimental.pallas import tpu as pltpu
from jax.sharding import PartitionSpec as P

F32 = jnp.float32
BF16 = jnp.bfloat16
ANY = pl.BlockSpec(memory_space=pl.ANY)
VMEM = pl.BlockSpec(memory_space=pltpu.VMEM)
HBM = pl.BlockSpec(memory_space=pltpu.HBM)
SMEM = pl.BlockSpec(memory_space=pltpu.SMEM)
NEAR_CHUNKS = (6, 6, 6, 7, 7)
MASKS = (1, 3, 7, 9, 25, 33, 97)


def split_rows(value):
    high = value.astype(BF16)
    low = (value - high.astype(F32)).astype(BF16)
    return jnp.concatenate([high, low], axis=0)


def join_rows(value):
    half = value.shape[0] // 2
    return value[:half] + value[half:]


def times(value, matrix):
    return join_rows(jnp.dot(split_rows(value), matrix, preferred_element_type=F32))


def times_transposed(value, matrix):
    dims = (((1,), (1,)), ((), ()))
    return join_rows(
        lax.dot_general(split_rows(value), matrix, dims, preferred_element_type=F32)
    )


def left_half(shape):
    return lax.broadcasted_iota(jnp.int32, shape, 1) < 64


def apart(pair):
    left = left_half(pair.shape)
    return jnp.concatenate([jnp.where(left, pair, 0.0), jnp.where(left, 0.0, pair)], axis=0)


def pick_nodes(position, matrices, picked):
    nodes = matrices.shape[2]
    count = 2 * 128
    row = lax.broadcasted_iota(jnp.int32, (8, nodes), 0)
    lane = lax.broadcasted_iota(jnp.int32, (8, nodes), 1)
    start = count - lax.shift_right_logical(jnp.full_like(row, count), row)
    wanted = start + lax.shift_right_logical(jnp.full_like(row, position), row)
    chosen = jnp.where(lane == wanted, 1.0, 0.0).astype(BF16)
    dims = (((1,), (1,)), ((), ()))
    for group in range(16):
        block = matrices[4 * group : 4 * group + 4].reshape(256, nodes)
        rows = lax.dot_general(chosen, block, dims, preferred_element_type=F32)
        shifted = pltpu.roll(rows, 64, 1)
        for half in range(2):
            lanes = slice(128 * half, 128 * half + 128)
            picked[pl.ds(4 * group + 2 * half, 8, stride=64), :] = rows[:, lanes]
            other = slice(128 * (1 - half), 128 * (1 - half) + 128)
            del other
            place = (128 * (half + 1)) % 256
            picked[pl.ds(4 * group + 2 * half + 1, 8, stride=64), :] = shifted[:, place : place + 128]


def in_hbm(*arrays):
    return [pltpu.with_memory_space_constraint(array, pltpu.HBM) for array in arrays]


def vmem(shape, dtype):
    return pltpu.VMEM(shape, dtype)


def vmem_like(array):
    return vmem(array.shape, array.dtype)


def tiles_like(tiles, count):
    return vmem((count,) + tiles.shape[1:], tiles.dtype)


def start_all(pairs, sems):
    copies = [pltpu.make_async_copy(source, target, sems.at[i]) for i, (source, target) in enumerate(pairs)]
    for copy in copies:
        copy.start()
    return copies


def params():
    return pltpu.CompilerParams(vmem_limit_bytes=24 * 2**20)


def cost(flops, size):
    return pl.CostEstimate(flops=flops, bytes_accessed=size, transcendentals=0)


def up_kernel(pos_ref, rhs_hbm, basis_hbm, trans_hbm, upper_hbm, upper_coup_hbm, coup_hbm,
              coef_ref, path_ref, upper_ref, rhs, basis, trans, upper_coup, coup,
              upper, picked, high, low, sems):
    copies = start_all(
        [
            (upper_hbm, upper),
            (rhs_hbm, rhs),
            (basis_hbm, basis),
            (trans_hbm, trans),
            (upper_coup_hbm, upper_coup),
            (coup_hbm, coup),
        ],
        sems,
    )
    copies[0].wait()
    pick_nodes(pos_ref[0], upper, picked)
    for copy in copies[1:4]:
        copy.wait()
    maps = None
    for level in range(6):
        matrix = picked[64 * level : 64 * level + 64, 0:64].astype(BF16)
        upper_ref[level] = matrix
        maps = matrix.astype(F32) if level == 0 else times(maps, matrix)
        lanes = slice(64 * (5 - level), 64 * (6 - level))
        head = maps.astype(BF16)
        high[:, lanes] = head
        low[:, lanes] = (maps - head.astype(F32)).astype(BF16)
    dims = (((1,), (1,)), ((), ()))
    current = []
    for pair in range(16):
        first = rhs[:, 512 * pair : 512 * pair + 256]
        second = rhs[:, 512 * pair + 256 : 512 * pair + 512]
        sources = jnp.concatenate([first, second], axis=0)
        both = lax.dot_general(
            sources, basis[2 * pair : 2 * pair + 2].reshape(128, 256), dims, preferred_element_type=F32
        )
        value = jnp.where(left_half((16, 128)), both[:16], both[16:])
        coef_ref[pair] = value
        current.append(value)
    base = 0
    while True:
        parents = [
            times(value, trans[2 * (base + i) : 2 * (base + i) + 2].reshape(128, 64))
            for i, value in enumerate(current)
        ]
        base += len(current)
        if len(parents) == 1:
            break
        current = [
            jnp.concatenate([parents[2 * i], parents[2 * i + 1]], axis=1) for i in range(len(parents) // 2)
        ]
        for i, value in enumerate(current):
            coef_ref[base + i] = value
    root = parents[0]
    path_ref[:, 384:448] = root
    path_ref[:, 0:384] = times(root, high[...]) + jnp.dot(
        root.astype(BF16), low[...], preferred_element_type=F32
    )
    for copy in copies[4:]:
        copy.wait()


def up_sweep(position, rhs, basis_t, local_transfer, upper_transfer_t, upper_coupling_t, local_coupling):
    return pl.pallas_call(
        up_kernel,
        out_shape=(
            vmem((31, 16, 128), F32),
            vmem((16, 448), F32),
            vmem((6, 64, 64), BF16),
            vmem_like(rhs),
            vmem_like(basis_t),
            vmem_like(local_transfer),
            vmem_like(upper_coupling_t),
            vmem_like(local_coupling),
        ),
        in_specs=[SMEM] + [HBM] * 6,
        out_specs=(VMEM,) * 8,
        scratch_shapes=[
            pltpu.VMEM(upper_transfer_t.shape, BF16),
            pltpu.VMEM((512, 128), F32),
            pltpu.VMEM((64, 384), BF16),
            pltpu.VMEM((64, 384), BF16),
            pltpu.SemaphoreType.DMA((6,)),
        ],
        compiler_params=params(),
        cost_estimate=cost(4 * 10**9, 2**20),
        name="up_sweep",
    )(
        position,
        *in_hbm(rhs, basis_t, local_transfer, upper_transfer_t, upper_coupling_t, local_coupling),
    )


def pick_kernel(pos_ref, order, upper, *refs):
    del order
    upper_ref, picked = refs[-2:]
    pick_nodes(pos_ref[0], upper, picked)
    for level in range(7):
        upper_ref[level] = picked[64 * level : 64 * level + 64, 0:64].astype(BF16)


def pick_couplings(position, order, upper_coupling_t, keep):
    return pl.pallas_call(
        pick_kernel,
        out_shape=vmem((7, 64, 64), BF16),
        in_specs=[SMEM, ANY, VMEM] + [VMEM] * len(keep),
        out_specs=VMEM,
        scratch_shapes=[pltpu.VMEM((512, 128), F32)],
        compiler_params=params(),
        cost_estimate=cost(6 * 10**9, 2**20),
        name="pick_couplings",
    )(position, order, upper_coupling_t, *keep)


def far_kernel(order, coef, coup, upper_trans, upper_coup, *refs):
    del order
    far_ref, high_ref, low_ref = refs[-3:]
    maps = upper_coup[6].astype(F32)
    for level in range(5, -1, -1):
        maps = times_transposed(maps, upper_trans[level])
        maps = jnp.concatenate([maps, upper_coup[level].astype(F32)], axis=0)
    high = maps.astype(BF16)
    high_ref[...] = high
    low_ref[...] = (maps - high.astype(F32)).astype(BF16)
    for pair in range(31):
        swapped = pltpu.roll(coef[pair], 64, 1)
        both = times(apart(swapped), coup[2 * pair : 2 * pair + 2].reshape(128, 64))
        far_ref[pair] = jnp.concatenate([both[:16], both[16:]], axis=1)


def far_fields(order, coef, coup, upper_trans, upper_coup, keep):
    return pl.pallas_call(
        far_kernel,
        out_shape=(vmem((31, 16, 128), F32), vmem((448, 64), BF16), vmem((448, 64), BF16)),
        in_specs=[ANY] + [VMEM] * (4 + len(keep)),
        out_specs=(VMEM,) * 3,
        compiler_params=params(),
        cost_estimate=cost(6 * 10**9, 2**20),
        name="far_fields",
    )(order, coef, coup, upper_trans, upper_coup, *keep)


def near_kernel(first, count, pos_ref, pairs_ref, order, inner, own, outer, across, tiles, *refs):
    del order
    out_ref = refs[-1]
    dims = (((1,), (1,)), ((), ()))
    position = pos_ref[0]
    row = lax.shift_right_logical(position, 3)
    for i in range(count):
        total = None
        for k in range(4):
            leaf = pairs_ref[k, first + i]
            holder = lax.shift_right_logical(leaf, 5)
            column = pl.ds(pl.multiple_of((leaf & 31) * 256, 256), 256)
            source = jnp.where(
                holder == position, own[:, column],
                jnp.where(
                    holder == position ^ 1, inner[:, column],
                    jnp.where(lax.shift_right_logical(holder, 3) == row, outer[:, column], across[:, column]),
                ),
            )
            part = lax.dot_general(source, tiles[first + i, k], dims, preferred_element_type=F32)
            total = part if total is None else total + part
        out_ref[:, 256 * i : 256 * i + 256] = total


def near_field(first, count, position, near_pairs_t, order, inner, own, outer, across, tiles, keep):
    return pl.pallas_call(
        functools.partial(near_kernel, first, count),
        out_shape=vmem((16, 256 * count), F32),
        in_specs=[SMEM, SMEM, ANY] + [VMEM] * (5 + len(keep)),
        out_specs=VMEM,
        compiler_params=params(),
        cost_estimate=cost(10**9, 2**20),
        name="near_field",
    )(position, near_pairs_t, order, inner, own, outer, across, tiles, *keep)


def down_kernel(*refs):
    siblings = refs[:7]
    high, low, far, trans, basis = refs[7:12]
    nearby = refs[12 : 12 + len(NEAR_CHUNKS)]
    out_ref = refs[12 + len(NEAR_CHUNKS)]
    field = jnp.zeros((16, 64), F32)
    for level in range(7):
        width = 64 * (7 - level)
        value = siblings[level][:, width - 64 : width]
        rows = slice(64 * (6 - level), 64 * (7 - level))
        field += times(value, high[rows])
        field += jnp.dot(value.astype(BF16), low[rows], preferred_element_type=F32)
    fields = [field]
    base = 31
    while len(fields) < 32:
        base -= len(fields)
        pairs = [
            far[base + i] + times_transposed(value, trans[2 * (base + i) : 2 * (base + i) + 2].reshape(128, 64))
            for i, value in enumerate(fields)
        ]
        if len(pairs) == 16:
            break
        fields = []
        for pair in pairs:
            fields += [pair[:, 0:64], pair[:, 64:128]]
    places = [(box, i) for box, count in enumerate(NEAR_CHUNKS) for i in range(count)]
    for leaf in range(0, 32, 2):
        both = times(apart(pairs[leaf // 2]), basis[leaf : leaf + 2].reshape(128, 256))
        for j in range(2):
            box, i = places[leaf + j]
            out_ref[:, 256 * (leaf + j) : 256 * (leaf + j) + 256] = (
                both[16 * j : 16 * j + 16] + nearby[box][:, 256 * i : 256 * i + 256]
            )


def down_sweep(siblings, high, low, far, local_transfer, basis_t, nearby):
    return pl.pallas_call(
        down_kernel,
        out_shape=jax.ShapeDtypeStruct((16, 8192), F32),
        in_specs=[VMEM] * (12 + len(nearby)),
        out_specs=VMEM,
        compiler_params=params(),
        cost_estimate=cost(3 * 10**9, 2**20),
        name="down_sweep",
    )(*siblings, high, low, far, local_transfer, basis_t, *nearby)


def onward(i, devices):
    if i % 8 == 0:
        return i + 8 if i + 8 < devices else i + 7
    if i % 8 == 7:
        return i - 8 if i >= 8 else i - 7
    return i + 1 if i % 2 else i - 1


def local(rhs, leaf_basis, near_tiles, near_pairs, local_transfer, local_coupling, upper_transfer, upper_coupling):
    devices = lax.axis_size("leaf")
    position = lax.axis_index("leaf").astype(jnp.int32)
    where = position.reshape(1)
    inward = [(i, i ^ 1) for i in range(devices)]
    outward = [(i, i // 8 * 8 + (i % 8 + 2 * (i % 2) - 1) % 8) for i in range(devices)]
    rows = [(i, onward(i, devices)) for i in range(devices)]
    near_pairs_t = jnp.transpose(near_pairs, (1, 0))
    outer = lax.ppermute(rhs, "leaf", outward)
    inner = lax.ppermute(rhs, "leaf", inward)
    coef, path, upper_trans, own, basis, trans, upper_coup, coup = up_sweep(
        where,
        rhs,
        jnp.transpose(leaf_basis, (0, 2, 1)),
        local_transfer,
        jnp.transpose(upper_transfer, (1, 2, 0)),
        jnp.transpose(upper_coupling, (1, 2, 0)),
        local_coupling,
    )

    nearby = []
    siblings = []
    first = 0
    for level in range(7):
        width = 64 * (7 - level)
        pairs = [(i, i ^ MASKS[level]) for i in range(devices)]
        received = lax.ppermute(path, "leaf", pairs)
        if level == 0:
            upper_coup = pick_couplings(where, path, upper_coup, [coef, coup, trans, basis])
            received, upper_coup = lax.optimization_barrier((received, upper_coup))
        elif level == 1:
            far, high, low = far_fields(path, coef, coup, upper_trans, upper_coup, [trans, basis])
            received, far = lax.optimization_barrier((received, far))
        else:
            count = NEAR_CHUNKS[level - 2]
            part = near_field(
                first, count, where, near_pairs_t, path, inner, own, outer, across, near_tiles, [far, trans, basis, high, low]
            )
            first += count
            received, part = lax.optimization_barrier((received, part))
            nearby.append(part)
        siblings.append(received)
        path = path[:, : width - 64] + received[:, : width - 64]
        if level == 0:
            outer, path = lax.optimization_barrier((outer, path))
            across = lax.ppermute(outer, "leaf", rows)
    return down_sweep(siblings, high, low, far, trans, basis, nearby)


def solution(mesh):
    return jax.shard_map(
        local,
        mesh=mesh,
        in_specs=(
            P(None, "leaf"),
            P("leaf", None, None),
            P("leaf", None, None, None),
            P("leaf", None),
            P("leaf", None, None),
            P("leaf", None, None),
            P(),
            P(),
        ),
        out_specs=P(None, "leaf"),
        check_vma=False,
    )
```

```python
import functools

import jax
import jax.numpy as jnp
from jax import lax
from jax.experimental import pallas as pl
from jax.experimental.pallas import tpu as pltpu
from jax.sharding import PartitionSpec as P

F32 = jnp.float32
BF16 = jnp.bfloat16
ANY = pl.BlockSpec(memory_space=pl.ANY)
VMEM = pl.BlockSpec(memory_space=pltpu.VMEM)
HBM = pl.BlockSpec(memory_space=pltpu.HBM)
SMEM = pl.BlockSpec(memory_space=pltpu.SMEM)
NEAR_CHUNKS = (8, 8, 8, 8)
FAR_LEVEL = 2
MASKS = (1, 3, 7, 9, 25, 33, 97)


def split_rows(value):
    high = value.astype(BF16)
    low = (value - high.astype(F32)).astype(BF16)
    return jnp.concatenate([high, low], axis=0)


def join_rows(value):
    half = value.shape[0] // 2
    return value[:half] + value[half:]


def times(value, matrix):
    return join_rows(jnp.dot(split_rows(value), matrix, preferred_element_type=F32))


def times_transposed(value, matrix):
    dims = (((1,), (1,)), ((), ()))
    return join_rows(
        lax.dot_general(split_rows(value), matrix, dims, preferred_element_type=F32)
    )


def left_half(shape):
    return lax.broadcasted_iota(jnp.int32, shape, 1) < 64


def apart(pair):
    left = left_half(pair.shape)
    return jnp.concatenate([jnp.where(left, pair, 0.0), jnp.where(left, 0.0, pair)], axis=0)


def pick_nodes(position, matrices, picked):
    nodes = matrices.shape[2]
    count = 2 * 128
    row = lax.broadcasted_iota(jnp.int32, (8, nodes), 0)
    lane = lax.broadcasted_iota(jnp.int32, (8, nodes), 1)
    start = count - lax.shift_right_logical(jnp.full_like(row, count), row)
    wanted = start + lax.shift_right_logical(jnp.full_like(row, position), row)
    chosen = jnp.where(lane == wanted, 1.0, 0.0).astype(BF16)
    dims = (((1,), (1,)), ((), ()))
    for group in range(16):
        block = matrices[4 * group : 4 * group + 4].reshape(256, nodes)
        rows = lax.dot_general(chosen, block, dims, preferred_element_type=F32)
        shifted = pltpu.roll(rows, 64, 1)
        for half in range(2):
            lanes = slice(128 * half, 128 * half + 128)
            picked[pl.ds(4 * group + 2 * half, 8, stride=64), :] = rows[:, lanes]
            other = slice(128 * (1 - half), 128 * (1 - half) + 128)
            del other
            place = (128 * (half + 1)) % 256
            picked[pl.ds(4 * group + 2 * half + 1, 8, stride=64), :] = shifted[:, place : place + 128]


def in_hbm(*arrays):
    return [pltpu.with_memory_space_constraint(array, pltpu.HBM) for array in arrays]


def vmem(shape, dtype):
    return pltpu.VMEM(shape, dtype)


def vmem_like(array):
    return vmem(array.shape, array.dtype)


def tiles_like(tiles, count):
    return vmem((count,) + tiles.shape[1:], tiles.dtype)


def start_pieces(pairs, sems):
    started = []
    at = 0
    for source, target, pieces in pairs:
        size = source.shape[0] // pieces
        group = []
        for i in range(pieces):
            span = slice(size * i, size * (i + 1) if i + 1 < pieces else source.shape[0])
            group.append(pltpu.make_async_copy(source.at[span], target.at[span], sems.at[at]))
            at += 1
        for copy in group:
            copy.start()
        started.append(group)
    return started


def finish(groups):
    for group in groups:
        for copy in group:
            copy.wait()


def params():
    return pltpu.CompilerParams(vmem_limit_bytes=24 * 2**20)


def cost(flops, size):
    return pl.CostEstimate(flops=flops, bytes_accessed=size, transcendentals=0)


def up_kernel(rhs_hbm, basis_hbm, trans_hbm, upper_hbm,
              coef_ref, path_ref, upper_ref, rhs, basis, trans,
              upper, picked, high, low, sems):
    copies = start_pieces(
        [
            (upper_hbm, upper, 8),
            (rhs_hbm, rhs, 1),
            (basis_hbm, basis, 4),
            (trans_hbm, trans, 4),
        ],
        sems,
    )
    finish(copies[:1])
    pick_nodes(lax.axis_index("leaf"), upper, picked)
    finish(copies[1:4])
    maps = None
    for level in range(6):
        matrix = picked[64 * level : 64 * level + 64, 0:64].astype(BF16)
        upper_ref[level] = matrix
        maps = matrix.astype(F32) if level == 0 else times(maps, matrix)
        lanes = slice(64 * (5 - level), 64 * (6 - level))
        head = maps.astype(BF16)
        high[:, lanes] = head
        low[:, lanes] = (maps - head.astype(F32)).astype(BF16)
    dims = (((1,), (1,)), ((), ()))
    current = []
    for pair in range(16):
        first = rhs[:, 512 * pair : 512 * pair + 256]
        second = rhs[:, 512 * pair + 256 : 512 * pair + 512]
        sources = jnp.concatenate([first, second], axis=0)
        both = lax.dot_general(
            sources, basis[2 * pair : 2 * pair + 2].reshape(128, 256), dims, preferred_element_type=F32
        )
        value = jnp.where(left_half((16, 128)), both[:16], both[16:])
        coef_ref[pair] = value
        current.append(value)
    base = 0
    while True:
        parents = [
            times(value, trans[2 * (base + i) : 2 * (base + i) + 2].reshape(128, 64))
            for i, value in enumerate(current)
        ]
        base += len(current)
        if len(parents) == 1:
            break
        current = [
            jnp.concatenate([parents[2 * i], parents[2 * i + 1]], axis=1) for i in range(len(parents) // 2)
        ]
        for i, value in enumerate(current):
            coef_ref[base + i] = value
    root = parents[0]
    path_ref[:, 384:448] = root
    path_ref[:, 0:384] = times(root, high[...]) + jnp.dot(
        root.astype(BF16), low[...], preferred_element_type=F32
    )


def up_sweep(rhs, basis_t, local_transfer, upper_transfer_t):
    return pl.pallas_call(
        up_kernel,
        out_shape=(
            vmem((31, 16, 128), F32),
            vmem((16, 448), F32),
            vmem((6, 64, 64), BF16),
            vmem_like(rhs),
            vmem_like(basis_t),
            vmem_like(local_transfer),
        ),
        in_specs=[HBM] * 4,
        out_specs=(VMEM,) * 6,
        scratch_shapes=[
            pltpu.VMEM(upper_transfer_t.shape, BF16),
            pltpu.VMEM((512, 128), F32),
            pltpu.VMEM((64, 384), BF16),
            pltpu.VMEM((64, 384), BF16),
            pltpu.SemaphoreType.DMA((17,)),
        ],
        compiler_params=params(),
        cost_estimate=cost(4 * 10**9, 2**20),
        name="up_sweep",
    )(
        *in_hbm(rhs, basis_t, local_transfer, upper_transfer_t),
    )


def pick_kernel(order, upper, *refs):
    del order
    upper_ref, picked = refs[-2:]
    pick_nodes(lax.axis_index("leaf"), upper, picked)
    for level in range(7):
        upper_ref[level] = picked[64 * level : 64 * level + 64, 0:64].astype(BF16)


def pick_couplings(order, upper_coupling_t, keep):
    return pl.pallas_call(
        pick_kernel,
        out_shape=vmem((7, 64, 64), BF16),
        in_specs=[ANY, VMEM] + [VMEM] * len(keep),
        out_specs=VMEM,
        scratch_shapes=[pltpu.VMEM((512, 128), F32)],
        compiler_params=params(),
        cost_estimate=cost(6 * 10**9, 2**20),
        name="pick_couplings",
    )(order, upper_coupling_t, *keep)


def far_kernel(order, coef, coup, upper_trans, upper_coup, *refs):
    del order
    far_ref, high_ref, low_ref = refs[-3:]
    maps = upper_coup[6].astype(F32)
    for level in range(5, -1, -1):
        maps = times_transposed(maps, upper_trans[level])
        maps = jnp.concatenate([maps, upper_coup[level].astype(F32)], axis=0)
    high = maps.astype(BF16)
    high_ref[...] = high
    low_ref[...] = (maps - high.astype(F32)).astype(BF16)
    for pair in range(31):
        swapped = pltpu.roll(coef[pair], 64, 1)
        both = times(apart(swapped), coup[2 * pair : 2 * pair + 2].reshape(128, 64))
        far_ref[pair] = jnp.concatenate([both[:16], both[16:]], axis=1)


def far_fields(order, coef, coup, upper_trans, upper_coup, keep):
    return pl.pallas_call(
        far_kernel,
        out_shape=(vmem((31, 16, 128), F32), vmem((448, 64), BF16), vmem((448, 64), BF16)),
        in_specs=[ANY] + [VMEM] * (4 + len(keep)),
        out_specs=(VMEM,) * 3,
        compiler_params=params(),
        cost_estimate=cost(6 * 10**9, 2**20),
        name="far_fields",
    )(order, coef, coup, upper_trans, upper_coup, *keep)


def near_kernel(first, count, pairs_ref, order, inner, own, outer, across, tiles, *refs):
    del order
    out_ref = refs[-1]
    dims = (((1,), (1,)), ((), ()))
    position = lax.axis_index("leaf")
    row = lax.shift_right_logical(position, 3)
    for i in range(count):
        total = None
        for k in range(4):
            leaf = pairs_ref[k, first + i]
            holder = lax.shift_right_logical(leaf, 5)
            column = pl.ds(pl.multiple_of((leaf & 31) * 256, 256), 256)
            source = jnp.where(
                holder == position, own[:, column],
                jnp.where(
                    holder == position ^ 1, inner[:, column],
                    jnp.where(lax.shift_right_logical(holder, 3) == row, outer[:, column], across[:, column]),
                ),
            )
            part = lax.dot_general(source, tiles[first + i, k], dims, preferred_element_type=F32)
            total = part if total is None else total + part
        out_ref[:, 256 * i : 256 * i + 256] = total


def near_field(first, count, near_pairs_t, order, inner, own, outer, across, tiles, keep):
    return pl.pallas_call(
        functools.partial(near_kernel, first, count),
        out_shape=vmem((16, 256 * count), F32),
        in_specs=[SMEM, ANY] + [VMEM] * (5 + len(keep)),
        out_specs=VMEM,
        compiler_params=params(),
        cost_estimate=cost(10**9, 2**20),
        name="near_field",
    )(near_pairs_t, order, inner, own, outer, across, tiles, *keep)


def down_kernel(*refs):
    siblings = refs[:7]
    high, low, far, trans, basis = refs[7:12]
    nearby = refs[12 : 12 + len(NEAR_CHUNKS)]
    out_hbm, out_ref, sems = refs[12 + len(NEAR_CHUNKS) :]
    field = jnp.zeros((16, 64), F32)
    for level in range(7):
        width = 64 * (7 - level)
        value = siblings[level][:, width - 64 : width]
        rows = slice(64 * (6 - level), 64 * (7 - level))
        field += times(value, high[rows])
        field += jnp.dot(value.astype(BF16), low[rows], preferred_element_type=F32)
    fields = [field]
    base = 31
    while len(fields) < 32:
        base -= len(fields)
        pairs = [
            far[base + i] + times_transposed(value, trans[2 * (base + i) : 2 * (base + i) + 2].reshape(128, 64))
            for i, value in enumerate(fields)
        ]
        if len(pairs) == 16:
            break
        fields = []
        for pair in pairs:
            fields += [pair[:, 0:64], pair[:, 64:128]]
    places = [(box, i) for box, count in enumerate(NEAR_CHUNKS) for i in range(count)]
    copies = []
    for leaf in range(0, 32, 2):
        both = times(apart(pairs[leaf // 2]), basis[leaf : leaf + 2].reshape(128, 256))
        for j in range(2):
            box, i = places[leaf + j]
            out_ref[:, 256 * (leaf + j) : 256 * (leaf + j) + 256] = (
                both[16 * j : 16 * j + 16] + nearby[box][:, 256 * i : 256 * i + 256]
            )
        if leaf % 8 == 6:
            lanes = pl.ds(256 * (leaf - 6), 2048)
            copies.append(pltpu.make_async_copy(out_ref.at[:, lanes], out_hbm.at[:, lanes], sems.at[leaf // 8]))
            copies[-1].start()
    for copy in copies:
        copy.wait()


def down_sweep(siblings, high, low, far, local_transfer, basis_t, nearby):
    return pl.pallas_call(
        down_kernel,
        out_shape=jax.ShapeDtypeStruct((16, 8192), F32),
        in_specs=[VMEM] * (12 + len(nearby)),
        out_specs=HBM,
        scratch_shapes=[pltpu.VMEM((16, 8192), F32), pltpu.SemaphoreType.DMA((4,))],
        compiler_params=params(),
        cost_estimate=cost(3 * 10**9, 2**20),
        name="down_sweep",
    )(*siblings, high, low, far, local_transfer, basis_t, *nearby)


def onward(i, devices):
    if i % 8 == 0:
        return i + 8 if i + 8 < devices else i + 7
    if i % 8 == 7:
        return i - 8 if i >= 8 else i - 7
    return i + 1 if i % 2 else i - 1


def local(rhs, leaf_basis, near_tiles, near_pairs, local_transfer, local_coupling, upper_transfer, upper_coupling):
    devices = lax.axis_size("leaf")
    inward = [(i, i ^ 1) for i in range(devices)]
    outward = [(i, i // 8 * 8 + (i % 8 + 2 * (i % 2) - 1) % 8) for i in range(devices)]
    rows = [(i, onward(i, devices)) for i in range(devices)]
    near_pairs_t = jnp.transpose(near_pairs, (1, 0))
    outer = lax.ppermute(rhs, "leaf", outward)
    inner = lax.ppermute(rhs, "leaf", inward)
    coef, path, upper_trans, own, basis, trans = up_sweep(
        rhs,
        jnp.transpose(leaf_basis, (0, 2, 1)),
        local_transfer,
        jnp.transpose(upper_transfer, (1, 2, 0)),
    )
    upper_coup = jnp.transpose(upper_coupling, (1, 2, 0))
    coup = local_coupling

    nearby = []
    siblings = []
    first = 0
    for level in range(7):
        width = 64 * (7 - level)
        pairs = [(i, i ^ MASKS[level]) for i in range(devices)]
        received = lax.ppermute(path, "leaf", pairs)
        if level == 1:
            upper_coup = pick_couplings(path, upper_coup, [coef, trans, basis])
            received, upper_coup = lax.optimization_barrier((received, upper_coup))
        elif level == FAR_LEVEL:
            far, high, low = far_fields(path, coef, coup, upper_trans, upper_coup, [trans, basis])
            received, far = lax.optimization_barrier((received, far))
        elif level > FAR_LEVEL:
            count = NEAR_CHUNKS[level - FAR_LEVEL - 1]
            part = near_field(
                first, count, near_pairs_t, path, inner, own, outer, across, near_tiles, [far, trans, basis, high, low]
            )
            first += count
            received, part = lax.optimization_barrier((received, part))
            nearby.append(part)
        siblings.append(received)
        path = path[:, : width - 64] + received[:, : width - 64]
        if level == 0:
            outer, path = lax.optimization_barrier((outer, path))
            across = lax.ppermute(outer, "leaf", rows)
    return down_sweep(siblings, high, low, far, trans, basis, nearby)


def solution(mesh):
    return jax.shard_map(
        local,
        mesh=mesh,
        in_specs=(
            P(None, "leaf"),
            P("leaf", None, None),
            P("leaf", None, None, None),
            P("leaf", None),
            P("leaf", None, None),
            P("leaf", None, None),
            P(),
            P(),
        ),
        out_specs=P(None, "leaf"),
        check_vma=False,
    )
```
